32 devices in a mesh: grp: 2 (over y), slab: 4 (over x, core), orb: 4 (over z).
Axes of the slice: x: 2, y: 2, z: 4, core: 2. Of those that a mesh axis runs over, the one named last changes fastest.
Arguments:
- mode_basis: bfloat16 [8, 5120, 256], P(('grp', 'slab'), 'orb'), parts along dimension 0, may hold values from -0.078125 to 0.078125
- onsite: bfloat16 [8, 2, 5120, 1280], P(('grp', 'slab'), None, 'orb'), parts along dimension 0, may hold values from -1.1953125 to 1.1953125
- onsite_cols: int32 [8, 32, 8], P(('grp', 'slab'), 'orb'), parts along dimension 0, may hold values from 0 to 31
- coupling: bfloat16 [8, 2, 5120, 1280], P(('grp', 'slab'), None, 'orb'), parts along dimension 0, may hold values from -0.29882812 to 0.29882812
- coupling_cols: int32 [8, 32, 8], P(('grp', 'slab'), 'orb'), parts along dimension 0, may hold values from 0 to 31
- energies: float32 [16], replicated, may hold values from -2 to 2
- owner: int32 [16], replicated, may hold values from 0 to 15, each once
Outputs:
- surface_gf: float32 [32, 2, 256, 256], P(('grp', 'slab', 'orb')), parts along dimension 0
- mode_dos: float32 [32, 4], P(('grp', 'slab', 'orb')), parts along dimension 0
The draws below stay inside these ranges and needn't reach their ends.
There are 2 independent parts, one for each index of `grp`. The reference program is written for one: setup_inputs(seed, part) draws one part's arguments, and reference() takes and returns one part's arrays. A program takes and returns all parts, laid end to end along the dimension named above; an argument that names none is the same for every part. Nothing has to cross between parts.
Inputs may be any that keep to these rules, and one draw needn't show every extreme that they name: `owner`: each slot index appears once.
All inputs are finite; a program needn't handle non-finite values.
Results may differ from the reference program's by a relative error of at most 0.0003.
The reference program's roundings to bfloat16 on the way count: a program that leaves them out, or rounds other values in their place, can miss the bound.
Values may be sent and summed in bfloat16 or wider, within the bound.
A program may use at most 128 MiB of HBM per device.

```python
import jax
import jax.numpy as jnp
from jax import lax

NORB = 5120
M = 256
BLK = 160
K = 8
NBLK = 32
SLABS = 4
ENERGIES = 16


def plant(values, own_key, least, high):
    extent = values.shape
    spot = [jax.random.randint(jax.random.fold_in(own_key, axis), (), 0, extent[axis]) for axis in range(len(extent))]
    values = values.at[tuple(spot)].set(least)
    longest = extent.index(max(extent))
    spot[longest] = (spot[longest] + 1) % extent[longest]
    return values.at[tuple(spot)].set(high)


def level_of(stream_key, shape, pieces, smallest, high):
    loudness = 1.0
    for dim, shards_of in pieces:
        steps = jax.random.uniform(jax.random.fold_in(jax.random.fold_in(stream_key, 6), dim), (shards_of,), jnp.float32, smallest / len(pieces), high / len(pieces))
        loudness = loudness * jnp.repeat(jnp.exp(steps), shape[dim] // shards_of).reshape((-1,) + (1,) * (len(shape) - 1 - dim))
    return loudness


def scatter_about(own_key, shape, scale, reach, pieces=(), kind=jnp.bfloat16):
    entries = jax.random.normal(own_key, shape, jnp.float32) * scale
    if len(pieces) > 0:
        entries = level_of(own_key, shape, pieces, -0.22, 0.18) * entries
    return jnp.clip(entries, min=-reach, max=reach).astype(kind)


def setup_inputs(seed: int = 0, part: int = 0) -> dict:
    splits = jax.random.split(jax.random.key(seed), 8)
    part_keys = jax.random.split(jax.random.fold_in(splits[7], part), 8)
    mode_basis = scatter_about(part_keys[0], (SLABS, NORB, M), NORB ** -0.5, 0.078125, ((0, 4), (1, 4)))
    onsite = scatter_about(part_keys[1], (SLABS, 2, NORB, K * BLK), 0.2, 1.1953125, ((0, 4), (2, 4)))
    onsite_cols = plant(jax.random.randint(part_keys[2], (SLABS, NBLK, K), 0, NBLK), jax.random.fold_in(part_keys[2], 1), 0, NBLK - 1).astype(jnp.int32)
    coupling = scatter_about(part_keys[3], (SLABS, 2, NORB, K * BLK), 0.05, 0.29882812, ((0, 4), (2, 4)))
    coupling_cols = plant(jax.random.randint(part_keys[4], (SLABS, NBLK, K), 0, NBLK), jax.random.fold_in(part_keys[4], 1), 0, NBLK - 1).astype(jnp.int32)
    energies = jnp.clip(jax.random.uniform(splits[5], (ENERGIES,), jnp.float32, -2.0, 2.0), -2.0, 2.0)
    owner = jax.random.permutation(splits[6], ENERGIES).astype(jnp.int32)
    return {"mode_basis": mode_basis, "onsite": onsite, "onsite_cols": onsite_cols, "coupling": coupling, "coupling_cols": coupling_cols, "energies": energies, "owner": owner}


broadening = 0.5
contact = 0.5

def matmul_exact(left, right):
    return jnp.matmul(left, right, precision=lax.Precision.HIGHEST)

def transpose_last(value):
    return jnp.swapaxes(value, -1, -2)

def complex_product(left_factor_real, left_factor_imaginary, right_re, right_im):
    real = matmul_exact(left_factor_real, right_re) - matmul_exact(left_factor_imaginary, right_im)
    imag = matmul_exact(left_factor_real, right_im) + matmul_exact(left_factor_imaginary, right_re)
    return (real, imag)

def adjoint_product(left_factor_real, left_factor_imaginary, right_re, right_im):
    real = matmul_exact(transpose_last(left_factor_real), right_re) + matmul_exact(transpose_last(left_factor_imaginary), right_im)
    imag = matmul_exact(transpose_last(left_factor_real), right_im) - matmul_exact(transpose_last(left_factor_imaginary), right_re)
    return (real, imag)

def invert(real, imag):
    gram_re, gram_im = adjoint_product(real, imag, real, imag)
    upper = jnp.concatenate([gram_re, -gram_im], -1)
    bottom = jnp.concatenate([gram_im, gram_re], -1)
    system = jnp.concatenate([upper, bottom], -2)
    factor = jnp.linalg.cholesky(system)
    rhs = jnp.concatenate([transpose_last(real), -transpose_last(imag)], -2)
    middle = lax.linalg.triangular_solve(factor, rhs, left_side=True, lower=True)
    result = lax.linalg.triangular_solve(factor, middle, left_side=True, lower=True, transpose_a=True)
    order = real.shape[-1]
    return (result[..., :order, :], result[..., order:, :])

def sweep(energy, blocks):
    order = blocks.shape[-1]
    ident = jnp.eye(order, dtype=blocks.dtype)
    shift_re = energy[:, None, None] * ident
    shift_im = broadening * ident
    wide_re, wide_im = adjoint_product(blocks[-1, 2], blocks[-1, 3], blocks[-1, 2], blocks[-1, 3])
    first_re = shift_re - blocks[0, 0] - contact * wide_im
    leading_imaginary = jnp.broadcast_to(shift_im - blocks[0, 1] + contact * wide_re, first_re.shape)
    green_re, green_im = invert(first_re, leading_imaginary)
    first_dos = -jnp.trace(green_im, axis1=-2, axis2=-1) / order

    def advance(carry, partial_blocks):
        prev_re, prev_im = carry
        hamil, hopping_coupling_matrix = partial_blocks
        prod_re, prod_im = complex_product(prev_re, prev_im, hopping_coupling_matrix[0], hopping_coupling_matrix[1])
        self_re, self_im = adjoint_product(hopping_coupling_matrix[0], hopping_coupling_matrix[1], prod_re, prod_im)
        next_re, next_im = invert(shift_re - hamil[0] - self_re, shift_im - hamil[1] - self_im)
        return ((next_re, next_im), -jnp.trace(next_im, axis1=-2, axis2=-1) / order)
    (green_re, green_im), rest = lax.scan(advance, (green_re, green_im), (blocks[1:, :2], blocks[:-1, 2:]))
    dos = jnp.concatenate([first_dos[None], rest], 0)
    return (jnp.stack([green_re, green_im], 1), jnp.transpose(dos))

def hermitian_blocks(raw):
    real = (raw[:, 0] + transpose_last(raw[:, 0])) / 2.0
    imag = (raw[:, 1] - transpose_last(raw[:, 1])) / 2.0
    return jnp.stack([real, imag, raw[:, 2], raw[:, 3]], 1)

def project(hamil, columns, mode_basis_row_block, basis_cols):
    table = basis_cols.reshape(NBLK, BLK, M)
    chosen = table[columns].reshape(NBLK, K * BLK, M)
    shaped = hamil.reshape(2, NBLK, BLK, K * BLK)
    matrix_product_result = jnp.einsum('cbrk,bkm->cbrm', shaped.astype(jnp.float32), chosen.astype(jnp.float32))
    matrix_product_result = matrix_product_result.astype(jnp.bfloat16).reshape(2, NORB, M)
    return jnp.einsum('nm,cnp->cmp', mode_basis_row_block.astype(jnp.float32), matrix_product_result.astype(jnp.float32))

def reference(mode_basis, onsite, onsite_cols, coupling, coupling_cols, energies, owner):
    partial_blocks = []
    for slab in range(SLABS):
        own = mode_basis[slab]
        follow = mode_basis[(slab + 1) % SLABS]
        partial_blocks.append(jnp.concatenate([project(onsite[slab], onsite_cols[slab], own, own), project(coupling[slab], coupling_cols[slab], own, follow)], 0))
    blocks = hermitian_blocks(jnp.stack(partial_blocks, 0))
    slot_energy = energies[owner]
    green, dos = sweep(slot_energy, blocks)
    return (green, dos)
```

```python
import jax
import jax.numpy as jnp
from jax import lax
from jax.experimental import pallas as pl
from jax.experimental.pallas import tpu as pltpu
from jax.sharding import PartitionSpec as P

M = 256
BLK = 160
K = 8
NBLK = 32


broadening = 0.5
contact = 0.5


def shifted(array, axis, by):
    size = lax.axis_size(axis)
    return lax.ppermute(array, axis, [(i, (i + by) % size) for i in range(size)])


HALF = 128
TILES = HALF // 8


def spread(tile, index):
    return jnp.take_along_axis(tile, index, axis=1, mode="promise_in_bounds")


def invert_half(re, im):
    lane = lax.broadcasted_iota(jnp.int32, (8, HALF), 1)
    sub = lax.broadcasted_iota(jnp.int32, (8, HALF), 0)

    def block_step(block, _):
        first = block * 8
        rows_re, rows_im = re[block], im[block]
        for j in range(8):
            index = jnp.full((8, HALF), first + j, jnp.int32)
            at = lane == index
            col_re, col_im = spread(rows_re, index), spread(rows_im, index)
            row_re = jnp.broadcast_to(rows_re[j : j + 1], (8, HALF))
            row_im = jnp.broadcast_to(rows_im[j : j + 1], (8, HALF))
            piv_re = jnp.broadcast_to(col_re[j : j + 1], (8, HALF))
            piv_im = jnp.broadcast_to(col_im[j : j + 1], (8, HALF))
            scale = 1.0 / (piv_re * piv_re + piv_im * piv_im)
            inv_re, inv_im = piv_re * scale, -piv_im * scale
            row_re, row_im = jnp.where(at, 1.0, row_re), jnp.where(at, 0.0, row_im)
            new_re = row_re * inv_re - row_im * inv_im
            new_im = row_re * inv_im + row_im * inv_re
            rest_re = jnp.where(at, 0.0, rows_re) - (col_re * new_re - col_im * new_im)
            rest_im = jnp.where(at, 0.0, rows_im) - (col_re * new_im + col_im * new_re)
            rows_re = jnp.where(sub == j, new_re, rest_re)
            rows_im = jnp.where(sub == j, new_im, rest_im)
        inside = (lane >= first) & (lane < first + 8)
        for half in range(2):
            ids = range(half * 8, half * 8 + 8)
            old = [(re[t], im[t]) for t in ids]
            acc = [(jnp.where(inside, 0.0, a), jnp.where(inside, 0.0, b)) for a, b in old]
            for j in range(8):
                index = jnp.full((8, HALF), first + j, jnp.int32)
                row_re = jnp.broadcast_to(rows_re[j : j + 1], (8, HALF))
                row_im = jnp.broadcast_to(rows_im[j : j + 1], (8, HALF))
                for n in range(8):
                    col_re, col_im = spread(old[n][0], index), spread(old[n][1], index)
                    acc[n] = (
                        acc[n][0] - col_re * row_re + col_im * row_im,
                        acc[n][1] - col_re * row_im - col_im * row_re,
                    )
            for n, t in enumerate(ids):
                re[t], im[t] = acc[n]
        re[block], im[block] = rows_re, rows_im
        return 0

    lax.fori_loop(0, TILES, block_step, 0)


def exact(left, right):
    return lax.dot_general(
        left,
        right,
        (((1,), (0,)), ((), ())),
        precision=lax.Precision.HIGHEST,
        preferred_element_type=jnp.float32,
    )


def times(left, right):
    width = right[0].shape[1]
    wide = jnp.concatenate([left[0], left[1]], 1)
    table = jnp.concatenate(
        [
            jnp.concatenate([right[0], right[1]], 1),
            jnp.concatenate([-right[1], right[0]], 1),
        ],
        0,
    )
    out = exact(wide, table)
    return out[:, :width], out[:, width:]


def adjoint(value):
    return value[0].T, -value[1].T


def sweep_kernel(energy_ref, blocks_ref, green_ref, dos_ref, work_re, work_im):
    eye = lax.broadcasted_iota(jnp.int32, (M, M), 0) == lax.broadcasted_iota(jnp.int32, (M, M), 1)
    energy = energy_ref[0]

    def inverse_of_half(re, im):
        work_re[...] = re.reshape(TILES, 8, HALF)
        work_im[...] = im.reshape(TILES, 8, HALF)
        invert_half(work_re, work_im)
        return work_re[...].reshape(HALF, HALF), work_im[...].reshape(HALF, HALF)

    def store(rows, columns, value):
        green_ref[0, rows, columns] = value[0]
        green_ref[1, rows, columns] = value[1]

    def load(rows, columns):
        return green_ref[0, rows, columns], green_ref[1, rows, columns]

    low, high = slice(0, HALF), slice(HALF, M)

    def step(s, _):
        lead = s == 0
        hop = jnp.where(lead, blocks_ref.shape[0] - 1, s - 1)
        t = (blocks_ref[hop, 2], blocks_ref[hop, 3])
        t_adj = adjoint(t)

        @pl.when(lead)
        def _():
            wide = times(t_adj, t)
            green_ref[0] = contact * wide[1]
            green_ref[1] = -contact * wide[0]

        @pl.when(jnp.logical_not(lead))
        def _():
            self_energy = times(t_adj, times((green_ref[0], green_ref[1]), t))
            green_ref[0] = self_energy[0]
            green_ref[1] = self_energy[1]

        raw_re, raw_im = blocks_ref[s, 0], blocks_ref[s, 1]
        ham_re = (raw_re + raw_re.T) / 2.0
        ham_im = (raw_im - raw_im.T) / 2.0
        green_ref[0] = jnp.where(eye, energy, 0.0) - ham_re - green_ref[0]
        green_ref[1] = jnp.where(eye, broadening, 0.0) - ham_im - green_ref[1]

        corner = inverse_of_half(*load(low, low))
        store(low, low, corner)
        upper = times(corner, load(low, high))
        drop = times(load(high, low), upper)
        last = load(high, high)
        schur = inverse_of_half(last[0] - drop[0], last[1] - drop[1])
        corner = load(low, low)
        left = times(load(high, low), corner)
        bottom = times(schur, left)
        right = times(upper, schur)
        fill = times(upper, bottom)
        store(high, high, schur)
        store(high, low, (-bottom[0], -bottom[1]))
        store(low, high, (-right[0], -right[1]))
        store(low, low, (corner[0] + fill[0], corner[1] + fill[1]))
        dos_ref[s] = -jnp.sum(jnp.where(eye, green_ref[1], 0.0)) / M
        return 0

    lax.fori_loop(0, blocks_ref.shape[0], step, 0)


def sweep_one(energy, blocks):
    green, dos = pl.pallas_call(
        sweep_kernel,
        out_shape=(
            jax.ShapeDtypeStruct((2, M, M), jnp.float32),
            jax.ShapeDtypeStruct((blocks.shape[0],), jnp.float32),
        ),
        in_specs=[
            pl.BlockSpec(memory_space=pltpu.SMEM),
            pl.BlockSpec(memory_space=pltpu.VMEM),
        ],
        out_specs=(
            pl.BlockSpec(memory_space=pltpu.VMEM),
            pl.BlockSpec(memory_space=pltpu.SMEM),
        ),
        scratch_shapes=[pltpu.VMEM((TILES, 8, HALF), jnp.float32)] * 2,
        compiler_params=pltpu.CompilerParams(vmem_limit_bytes=40 * 1024 * 1024),
    )(energy.reshape(1), blocks)
    return green, dos


def sweep(energy, blocks):
    pairs = [sweep_one(energy[e], blocks) for e in range(energy.shape[0])]
    return jnp.stack([p[0] for p in pairs]), jnp.stack([p[1] for p in pairs])


def pick_blocks(table, index):
    return table[index]


def project(hamil, columns, mode_basis_row_block, basis_cols):
    slab_count = hamil.shape[0]
    row_count = hamil.shape[2]
    block_count = columns.shape[1]
    table = basis_cols.reshape(slab_count, NBLK, BLK, M)
    chosen = jax.vmap(pick_blocks)(table, columns).reshape(slab_count, block_count, K * BLK, M)
    shaped = hamil.reshape(slab_count, 2, block_count, BLK, K * BLK)
    matrix_product_result = jnp.einsum(
        "scbrk,sbkm->scbrm", shaped, chosen, preferred_element_type=jnp.float32
    )
    matrix_product_result = matrix_product_result.astype(jnp.bfloat16).reshape(
        slab_count, 2, row_count, M
    )
    return jnp.einsum(
        "atw,abti->abwi",
        mode_basis_row_block,
        matrix_product_result,
        preferred_element_type=jnp.float32,
    )


def on_device(mode_basis, onsite, onsite_cols, coupling, coupling_cols, energies, owner):
    slab_count = mode_basis.shape[0]
    own_all = lax.all_gather(mode_basis, "orb", axis=1, tiled=True)
    moved_rows = shifted(mode_basis, "slab", -1)
    first_next = lax.all_gather(moved_rows, "orb", axis=1, tiled=True)
    next_all = jnp.concatenate([own_all[1:], first_next], 0)
    onsite_part = project(onsite, onsite_cols, mode_basis, own_all)
    coupling_part = project(coupling, coupling_cols, mode_basis, next_all)
    partial_value = jnp.concatenate([onsite_part, coupling_part], 1).reshape(slab_count, 4 * M * M)
    summed = lax.psum(partial_value, "orb")
    collected = lax.all_gather(summed, "slab", axis=0, tiled=True)
    blocks = collected.reshape(-1, 4, M, M)
    energy_count = energies.shape[0]
    per_device = energy_count // lax.axis_size(("slab", "orb"))
    slot_index = lax.axis_index(("slab", "orb")) * per_device + jnp.arange(
        per_device, dtype=jnp.int32
    )
    positions = jnp.arange(energy_count, dtype=jnp.int32)
    selected_owner_device = jnp.sum(
        jnp.where(positions[None, :] == slot_index[:, None], owner[None, :], 0), 1
    )
    slot_energy = jnp.sum(
        jnp.where(positions[None, :] == selected_owner_device[:, None], energies[None, :], 0.0), 1
    )
    green, dos = sweep(slot_energy, blocks)
    return (green, dos)


def solution(mesh):
    in_specs = (
        P(("grp", "slab"), "orb", None),
        P(("grp", "slab"), None, "orb", None),
        P(("grp", "slab"), "orb", None),
        P(("grp", "slab"), None, "orb", None),
        P(("grp", "slab"), "orb", None),
        P(),
        P(),
    )
    out_specs = (P(("grp", "slab", "orb"), None, None, None), P(("grp", "slab", "orb"), None))
    return jax.shard_map(
        on_device, mesh=mesh, in_specs=in_specs, out_specs=out_specs, check_vma=False
    )
```

```python
import jax
import jax.numpy as jnp
from jax import lax
from jax.experimental import pallas as pl
from jax.experimental.pallas import tpu as pltpu
from jax.sharding import PartitionSpec as P

M = 256
BLK = 160
K = 8
NBLK = 32


broadening = 0.5
contact = 0.5


def shifted(array, axis, by):
    size = lax.axis_size(axis)
    return lax.ppermute(array, axis, [(i, (i + by) % size) for i in range(size)])


HALF = 128
TILES = HALF // 8


def spread(tile, index):
    return jnp.take_along_axis(tile, index, axis=1, mode="promise_in_bounds")


def invert_half(re, im):
    lane = lax.broadcasted_iota(jnp.int32, (8, HALF), 1)
    sub = lax.broadcasted_iota(jnp.int32, (8, HALF), 0)

    def eliminate(first, rows_re, rows_im):
        cols = []
        for j in range(8):
            index = jnp.full((8, HALF), first + j, jnp.int32)
            cols.append((spread(rows_re, index), spread(rows_im, index)))
        for j in range(8):
            at = lane == first + j
            here = sub == j
            col_re, col_im = cols[j]
            row_re = jnp.broadcast_to(rows_re[j : j + 1], (8, HALF))
            row_im = jnp.broadcast_to(rows_im[j : j + 1], (8, HALF))
            piv_re = jnp.broadcast_to(col_re[j : j + 1], (8, HALF))
            piv_im = jnp.broadcast_to(col_im[j : j + 1], (8, HALF))
            scale = 1.0 / (piv_re * piv_re + piv_im * piv_im)
            inv_re, inv_im = piv_re * scale, -piv_im * scale

            def reduced(old_re, old_im, row_re, row_im):
                new_re = row_re * inv_re - row_im * inv_im
                new_im = row_re * inv_im + row_im * inv_re
                rest_re = old_re - (col_re * new_re - col_im * new_im)
                rest_im = old_im - (col_re * new_im + col_im * new_re)
                return jnp.where(here, new_re, rest_re), jnp.where(here, new_im, rest_im)

            for m in range(j + 1, 8):
                old_re, old_im = cols[m]
                cols[m] = reduced(
                    old_re,
                    old_im,
                    jnp.broadcast_to(old_re[j : j + 1], (8, HALF)),
                    jnp.broadcast_to(old_im[j : j + 1], (8, HALF)),
                )
            rows_re, rows_im = reduced(
                jnp.where(at, 0.0, rows_re),
                jnp.where(at, 0.0, rows_im),
                jnp.where(at, 1.0, row_re),
                jnp.where(at, 0.0, row_im),
            )
        return rows_re, rows_im

    def update(first, old, panel):
        inside = (lane >= first) & (lane < first + 8)
        acc = [(jnp.where(inside, 0.0, a), jnp.where(inside, 0.0, b)) for a, b in old]
        for j in range(8):
            index = jnp.full((8, HALF), first + j, jnp.int32)
            row_re = jnp.broadcast_to(panel[0][j : j + 1], (8, HALF))
            row_im = jnp.broadcast_to(panel[1][j : j + 1], (8, HALF))
            for n in range(len(old)):
                col_re, col_im = spread(old[n][0], index), spread(old[n][1], index)
                acc[n] = (
                    acc[n][0] - col_re * row_re + col_im * row_im,
                    acc[n][1] - col_re * row_im - col_im * row_re,
                )
        return acc

    def block_step(block, panel):
        first = block * 8
        after = jnp.minimum(block + 1, TILES - 1)
        ahead = update(first, [(re[after], im[after])], panel)[0]
        following = eliminate(after * 8, *ahead)
        for part in range(0, TILES, 8):
            ids = range(part, part + 8)
            fresh = update(first, [(re[t], im[t]) for t in ids], panel)
            for n, t in enumerate(ids):
                re[t], im[t] = fresh[n]
        re[block], im[block] = panel
        return following

    lax.fori_loop(0, TILES, block_step, eliminate(0, re[0], im[0]))


def exact(left, right):
    return lax.dot_general(
        left,
        right,
        (((1,), (0,)), ((), ())),
        precision=lax.Precision.HIGHEST,
        preferred_element_type=jnp.float32,
    )


def times(left, right):
    width = right[0].shape[1]
    wide = jnp.concatenate([left[0], left[1]], 1)
    table = jnp.concatenate(
        [
            jnp.concatenate([right[0], right[1]], 1),
            jnp.concatenate([-right[1], right[0]], 1),
        ],
        0,
    )
    out = exact(wide, table)
    return out[:, :width], out[:, width:]


def adjoint(value):
    return value[0].T, -value[1].T


def sweep_kernel(energy_ref, hamil_ref, hopping_ref, green_ref, dos_ref, work_re, work_im):
    eye = lax.broadcasted_iota(jnp.int32, (M, M), 0) == lax.broadcasted_iota(jnp.int32, (M, M), 1)
    energy = energy_ref[0]

    def inverse_of_half(re, im):
        work_re[...] = re.reshape(TILES, 8, HALF)
        work_im[...] = im.reshape(TILES, 8, HALF)
        invert_half(work_re, work_im)
        return work_re[...].reshape(HALF, HALF), work_im[...].reshape(HALF, HALF)

    def store(rows, columns, value):
        green_ref[0, rows, columns] = value[0]
        green_ref[1, rows, columns] = value[1]

    def load(rows, columns):
        return green_ref[0, rows, columns], green_ref[1, rows, columns]

    low, high = slice(0, HALF), slice(HALF, M)

    def step(s, _):
        lead = s == 0
        hop = jnp.where(lead, hamil_ref.shape[0] - 1, s - 1)
        t = (hopping_ref[hop, 0], hopping_ref[hop, 1])
        t_adj = adjoint(t)

        @pl.when(lead)
        def _():
            wide = times(t_adj, t)
            green_ref[0] = contact * wide[1]
            green_ref[1] = -contact * wide[0]

        @pl.when(jnp.logical_not(lead))
        def _():
            self_energy = times(t_adj, times((green_ref[0], green_ref[1]), t))
            green_ref[0] = self_energy[0]
            green_ref[1] = self_energy[1]

        raw_re, raw_im = hamil_ref[s, 0], hamil_ref[s, 1]
        ham_re = (raw_re + raw_re.T) / 2.0
        ham_im = (raw_im - raw_im.T) / 2.0
        green_ref[0] = jnp.where(eye, energy, 0.0) - ham_re - green_ref[0]
        green_ref[1] = jnp.where(eye, broadening, 0.0) - ham_im - green_ref[1]

        corner = inverse_of_half(*load(low, low))
        store(low, low, corner)
        upper = times(corner, load(low, high))
        drop = times(load(high, low), upper)
        last = load(high, high)
        schur = inverse_of_half(last[0] - drop[0], last[1] - drop[1])
        corner = load(low, low)
        left = times(load(high, low), corner)
        bottom = times(schur, left)
        right = times(upper, schur)
        fill = times(upper, bottom)
        store(high, high, schur)
        store(high, low, (-bottom[0], -bottom[1]))
        store(low, high, (-right[0], -right[1]))
        store(low, low, (corner[0] + fill[0], corner[1] + fill[1]))
        dos_ref[s] = -jnp.sum(jnp.where(eye, green_ref[1], 0.0)) / M
        return 0

    lax.fori_loop(0, hamil_ref.shape[0], step, 0)


def sweep_one(energy, hamil, hopping):
    green, dos = pl.pallas_call(
        sweep_kernel,
        out_shape=(
            jax.ShapeDtypeStruct((2, M, M), jnp.float32),
            jax.ShapeDtypeStruct((hamil.shape[0],), jnp.float32),
        ),
        in_specs=[
            pl.BlockSpec(memory_space=pltpu.SMEM),
            pl.BlockSpec(memory_space=pltpu.VMEM),
            pl.BlockSpec(memory_space=pltpu.VMEM),
        ],
        out_specs=(
            pl.BlockSpec(memory_space=pltpu.VMEM),
            pl.BlockSpec(memory_space=pltpu.SMEM),
        ),
        scratch_shapes=[pltpu.VMEM((TILES, 8, HALF), jnp.float32)] * 2,
        compiler_params=pltpu.CompilerParams(vmem_limit_bytes=40 * 1024 * 1024),
    )(energy.reshape(1), hamil, hopping)
    return green, dos


def sweep(energy, hamil, hopping):
    pairs = [sweep_one(energy[e], hamil, hopping) for e in range(energy.shape[0])]
    return jnp.stack([p[0] for p in pairs]), jnp.stack([p[1] for p in pairs])


def pick_blocks(table, index):
    return table[index]


def project(hamil, columns, mode_basis_row_block, basis_cols):
    slab_count = hamil.shape[0]
    row_count = hamil.shape[2]
    block_count = columns.shape[1]
    width = basis_cols.shape[2]
    table = basis_cols.reshape(slab_count, NBLK, BLK, width)
    chosen = jax.vmap(pick_blocks)(table, columns).reshape(slab_count, block_count, K * BLK, width)
    shaped = hamil.reshape(slab_count, 2, block_count, BLK, K * BLK)
    matrix_product_result = jnp.einsum(
        "scbrk,sbkm->scbrm", shaped, chosen, preferred_element_type=jnp.float32
    )
    matrix_product_result = matrix_product_result.astype(jnp.bfloat16).reshape(
        slab_count, 2, row_count, width
    )
    return jnp.einsum(
        "atw,abti->abwi",
        mode_basis_row_block,
        matrix_product_result,
        preferred_element_type=jnp.float32,
    )


def share(partial_value):
    slab_count = partial_value.shape[0]
    rows = partial_value.reshape(slab_count, 2 * M, M)
    own = lax.psum_scatter(rows, "orb", scatter_dimension=1, tiled=True)
    every = lax.all_gather(own, ("slab", "orb"), axis=0, tiled=False)
    every = every.reshape(lax.axis_size("slab"), lax.axis_size("orb"), slab_count, -1, M)
    return jnp.swapaxes(every, 1, 2).reshape(-1, 2, M, M)


def on_device(mode_basis, onsite, onsite_cols, coupling, coupling_cols, energies, owner):
    halves = [mode_basis[:, :, : M // 2], mode_basis[:, :, M // 2 :]]
    own = [lax.all_gather(half, "orb", axis=1, tiled=True) for half in halves]
    following = [
        jnp.concatenate([all_rows[1:], shifted(all_rows[:1], "slab", -1)], 0) for all_rows in own
    ]
    onsite_part = jnp.concatenate(
        [project(onsite, onsite_cols, mode_basis, half) for half in own], -1
    )
    hamil = share(onsite_part)
    coupling_part = jnp.concatenate(
        [project(coupling, coupling_cols, mode_basis, half) for half in following], -1
    )
    hopping = share(coupling_part)
    energy_count = energies.shape[0]
    per_device = energy_count // lax.axis_size(("slab", "orb"))
    slot_index = lax.axis_index(("slab", "orb")) * per_device + jnp.arange(
        per_device, dtype=jnp.int32
    )
    positions = jnp.arange(energy_count, dtype=jnp.int32)
    selected_owner_device = jnp.sum(
        jnp.where(positions[None, :] == slot_index[:, None], owner[None, :], 0), 1
    )
    slot_energy = jnp.sum(
        jnp.where(positions[None, :] == selected_owner_device[:, None], energies[None, :], 0.0), 1
    )
    green, dos = sweep(slot_energy, hamil, hopping)
    return (green, dos)


def solution(mesh):
    in_specs = (
        P(("grp", "slab"), "orb", None),
        P(("grp", "slab"), None, "orb", None),
        P(("grp", "slab"), "orb", None),
        P(("grp", "slab"), None, "orb", None),
        P(("grp", "slab"), "orb", None),
        P(),
        P(),
    )
    out_specs = (P(("grp", "slab", "orb"), None, None, None), P(("grp", "slab", "orb"), None))
    return jax.shard_map(
        on_device, mesh=mesh, in_specs=in_specs, out_specs=out_specs, check_vma=False
    )
```

```python
import jax
import jax.numpy as jnp
from jax import lax
from jax.experimental import pallas as pl
from jax.experimental.pallas import tpu as pltpu
from jax.sharding import PartitionSpec as P

M = 256
BLK = 160
K = 8
NBLK = 32


broadening = 0.5
contact = 0.5


def shifted(array, axis, by):
    size = lax.axis_size(axis)
    return lax.ppermute(array, axis, [(i, (i + by) % size) for i in range(size)])


HALF = 128
TILES = HALF // 8


def spread(tile, index):
    return jnp.take_along_axis(tile, index, axis=1, mode="promise_in_bounds")


def invert_half(re, im):
    lane = lax.broadcasted_iota(jnp.int32, (8, HALF), 1)
    sub = lax.broadcasted_iota(jnp.int32, (8, HALF), 0)

    def eliminate(first, rows_re, rows_im):
        cols = []
        for j in range(8):
            index = jnp.full((8, HALF), first + j, jnp.int32)
            cols.append((spread(rows_re, index), spread(rows_im, index)))
        for j in range(8):
            at = lane == first + j
            here = sub == j
            col_re, col_im = cols[j]
            row_re = jnp.broadcast_to(rows_re[j : j + 1], (8, HALF))
            row_im = jnp.broadcast_to(rows_im[j : j + 1], (8, HALF))
            piv_re = jnp.broadcast_to(col_re[j : j + 1], (8, HALF))
            piv_im = jnp.broadcast_to(col_im[j : j + 1], (8, HALF))
            scale = 1.0 / (piv_re * piv_re + piv_im * piv_im)
            inv_re, inv_im = piv_re * scale, -piv_im * scale

            def reduced(old_re, old_im, row_re, row_im):
                new_re = row_re * inv_re - row_im * inv_im
                new_im = row_re * inv_im + row_im * inv_re
                rest_re = old_re - (col_re * new_re - col_im * new_im)
                rest_im = old_im - (col_re * new_im + col_im * new_re)
                return jnp.where(here, new_re, rest_re), jnp.where(here, new_im, rest_im)

            for m in range(j + 1, 8):
                old_re, old_im = cols[m]
                cols[m] = reduced(
                    old_re,
                    old_im,
                    jnp.broadcast_to(old_re[j : j + 1], (8, HALF)),
                    jnp.broadcast_to(old_im[j : j + 1], (8, HALF)),
                )
            rows_re, rows_im = reduced(
                jnp.where(at, 0.0, rows_re),
                jnp.where(at, 0.0, rows_im),
                jnp.where(at, 1.0, row_re),
                jnp.where(at, 0.0, row_im),
            )
        return rows_re, rows_im

    def update(first, old, panel):
        inside = (lane >= first) & (lane < first + 8)
        acc = [(jnp.where(inside, 0.0, a), jnp.where(inside, 0.0, b)) for a, b in old]
        for j in range(8):
            index = jnp.full((8, HALF), first + j, jnp.int32)
            row_re = jnp.broadcast_to(panel[0][j : j + 1], (8, HALF))
            row_im = jnp.broadcast_to(panel[1][j : j + 1], (8, HALF))
            for n in range(len(old)):
                col_re, col_im = spread(old[n][0], index), spread(old[n][1], index)
                acc[n] = (
                    acc[n][0] - col_re * row_re + col_im * row_im,
                    acc[n][1] - col_re * row_im - col_im * row_re,
                )
        return acc

    def block_step(block, panel):
        first = block * 8
        after = jnp.minimum(block + 1, TILES - 1)
        ahead = update(first, [(re[after], im[after])], panel)[0]
        following = eliminate(after * 8, *ahead)
        for part in range(0, TILES, 8):
            ids = range(part, part + 8)
            fresh = update(first, [(re[t], im[t]) for t in ids], panel)
            for n, t in enumerate(ids):
                re[t], im[t] = fresh[n]
        re[block], im[block] = panel
        return following

    lax.fori_loop(0, TILES, block_step, eliminate(0, re[0], im[0]))


def exact(left, right):
    return lax.dot_general(
        left,
        right,
        (((1,), (0,)), ((), ())),
        precision=lax.Precision.HIGHEST,
        preferred_element_type=jnp.float32,
    )


def times(left, right):
    width = right[0].shape[1]
    wide = jnp.concatenate([left[0], left[1]], 1)
    table = jnp.concatenate(
        [
            jnp.concatenate([right[0], right[1]], 1),
            jnp.concatenate([-right[1], right[0]], 1),
        ],
        0,
    )
    out = exact(wide, table)
    return out[:, :width], out[:, width:]


def adjoint(value):
    return value[0].T, -value[1].T


def sweep_kernel(energy_ref, places_ref, hamil_ref, hopping_ref, green_ref, dos_ref, work_re, work_im):
    eye = lax.broadcasted_iota(jnp.int32, (M, M), 0) == lax.broadcasted_iota(jnp.int32, (M, M), 1)
    energy = energy_ref[0]

    def inverse_of_half(re, im):
        work_re[...] = re.reshape(TILES, 8, HALF)
        work_im[...] = im.reshape(TILES, 8, HALF)
        invert_half(work_re, work_im)
        return work_re[...].reshape(HALF, HALF), work_im[...].reshape(HALF, HALF)

    def store(rows, columns, value):
        green_ref[0, rows, columns] = value[0]
        green_ref[1, rows, columns] = value[1]

    def load(rows, columns):
        return green_ref[0, rows, columns], green_ref[1, rows, columns]

    low, high = slice(0, HALF), slice(HALF, M)

    def step(s, _):
        lead = s == 0
        hop = places_ref[jnp.where(lead, hamil_ref.shape[0] - 1, s - 1)]
        here = places_ref[s]
        t = (hopping_ref[hop, 0], hopping_ref[hop, 1])
        t_adj = adjoint(t)

        @pl.when(lead)
        def _():
            wide = times(t_adj, t)
            green_ref[0] = contact * wide[1]
            green_ref[1] = -contact * wide[0]

        @pl.when(jnp.logical_not(lead))
        def _():
            self_energy = times(t_adj, times((green_ref[0], green_ref[1]), t))
            green_ref[0] = self_energy[0]
            green_ref[1] = self_energy[1]

        raw_re, raw_im = hamil_ref[here, 0], hamil_ref[here, 1]
        ham_re = (raw_re + raw_re.T) / 2.0
        ham_im = (raw_im - raw_im.T) / 2.0
        green_ref[0] = jnp.where(eye, energy, 0.0) - ham_re - green_ref[0]
        green_ref[1] = jnp.where(eye, broadening, 0.0) - ham_im - green_ref[1]

        corner = inverse_of_half(*load(low, low))
        store(low, low, corner)
        upper = times(corner, load(low, high))
        drop = times(load(high, low), upper)
        last = load(high, high)
        schur = inverse_of_half(last[0] - drop[0], last[1] - drop[1])
        corner = load(low, low)
        left = times(load(high, low), corner)
        bottom = times(schur, left)
        right = times(upper, schur)
        fill = times(upper, bottom)
        store(high, high, schur)
        store(high, low, (-bottom[0], -bottom[1]))
        store(low, high, (-right[0], -right[1]))
        store(low, low, (corner[0] + fill[0], corner[1] + fill[1]))
        dos_ref[s] = -jnp.sum(jnp.where(eye, green_ref[1], 0.0)) / M
        return 0

    lax.fori_loop(0, hamil_ref.shape[0], step, 0)


def sweep_one(energy, places, hamil, hopping):
    green, dos = pl.pallas_call(
        sweep_kernel,
        out_shape=(
            jax.ShapeDtypeStruct((2, M, M), jnp.float32),
            jax.ShapeDtypeStruct((hamil.shape[0],), jnp.float32),
        ),
        in_specs=[
            pl.BlockSpec(memory_space=pltpu.SMEM),
            pl.BlockSpec(memory_space=pltpu.SMEM),
            pl.BlockSpec(memory_space=pltpu.VMEM),
            pl.BlockSpec(memory_space=pltpu.VMEM),
        ],
        out_specs=(
            pl.BlockSpec(memory_space=pltpu.VMEM),
            pl.BlockSpec(memory_space=pltpu.SMEM),
        ),
        scratch_shapes=[pltpu.VMEM((TILES, 8, HALF), jnp.float32)] * 2,
        compiler_params=pltpu.CompilerParams(vmem_limit_bytes=40 * 1024 * 1024),
    )(energy.reshape(1), places, hamil, hopping)
    return green, dos


def sweep(energy, places, hamil, hopping):
    pairs = [sweep_one(energy[e], places, hamil, hopping) for e in range(energy.shape[0])]
    return jnp.stack([p[0] for p in pairs]), jnp.stack([p[1] for p in pairs])


def pick_blocks(table, index):
    return table[index]


def project(hamil, columns, mode_basis_row_block, basis_cols):
    slab_count = hamil.shape[0]
    row_count = hamil.shape[2]
    block_count = columns.shape[1]
    width = basis_cols.shape[2]
    table = basis_cols.reshape(slab_count, NBLK, BLK, width)
    chosen = jax.vmap(pick_blocks)(table, columns).reshape(slab_count, block_count, K * BLK, width)
    shaped = hamil.reshape(slab_count, 2, block_count, BLK, K * BLK)
    matrix_product_result = jnp.einsum(
        "scbrk,sbkm->scbrm", shaped, chosen, preferred_element_type=jnp.float32
    )
    matrix_product_result = matrix_product_result.astype(jnp.bfloat16).reshape(
        slab_count, 2, row_count, width
    )
    return jnp.einsum(
        "atw,abti->abwi",
        mode_basis_row_block,
        matrix_product_result,
        preferred_element_type=jnp.float32,
    )


def share(partial_value):
    slab_count = partial_value.shape[0]
    size = lax.axis_size("orb")
    if size <= 8:
        me = lax.axis_index("orb")
        pieces = partial_value.reshape(slab_count, size, 2 * M // size, M)

        def piece(which):
            return lax.dynamic_index_in_dim(pieces, lax.rem(which, size), 1, keepdims=True)

        own = piece(me)
        for by in [shifted(piece(me + k), "orb", k) for k in range(1, size)]:
            own = own + by
        moved = [own] + [shifted(own, "orb", k) for k in range(1, size)]
        summed = jnp.zeros_like(pieces)
        for k in range(size):
            place = lax.rem(me + size - k, size)
            summed = lax.dynamic_update_slice_in_dim(summed, moved[k], place, 1)
    else:
        summed = lax.psum(partial_value, "orb")
    blocks = summed.reshape(slab_count, 2, M, M)
    slabs = lax.axis_size("slab")
    if slabs & (slabs - 1):
        return lax.all_gather(blocks, "slab", axis=0, tiled=True)
    bit = slabs // 2
    while bit:
        other = lax.ppermute(blocks, "slab", [(i, i ^ bit) for i in range(slabs)])
        blocks = jnp.concatenate([blocks, other], 0)
        bit //= 2
    return blocks


def slab_places(slab_count):
    slabs = lax.axis_size("slab")
    device = jnp.arange(slabs, dtype=jnp.int32)
    if slabs & (slabs - 1) == 0:
        apart = device ^ lax.axis_index("slab")
        device = jnp.zeros_like(apart)
        bit, weight = slabs // 2, 1
        while bit:
            device = device + jnp.where((apart & bit) != 0, weight, 0)
            bit, weight = bit // 2, weight * 2
    inside = jnp.arange(slab_count, dtype=jnp.int32)
    return (device[:, None] * slab_count + inside[None, :]).reshape(-1)


def on_device(mode_basis, onsite, onsite_cols, coupling, coupling_cols, energies, owner):
    halves = [mode_basis[:, :, : M // 2], mode_basis[:, :, M // 2 :]]
    own = [lax.all_gather(half, "orb", axis=1, tiled=True) for half in halves]
    following = [
        jnp.concatenate([all_rows[1:], shifted(all_rows[:1], "slab", -1)], 0) for all_rows in own
    ]
    onsite_part = jnp.concatenate(
        [project(onsite, onsite_cols, mode_basis, half) for half in own], -1
    )
    hamil = share(onsite_part)
    coupling_part = jnp.concatenate(
        [project(coupling, coupling_cols, mode_basis, half) for half in following], -1
    )
    hopping = share(coupling_part)
    places = slab_places(mode_basis.shape[0])
    energy_count = energies.shape[0]
    per_device = energy_count // lax.axis_size(("slab", "orb"))
    slot_index = lax.axis_index(("slab", "orb")) * per_device + jnp.arange(
        per_device, dtype=jnp.int32
    )
    positions = jnp.arange(energy_count, dtype=jnp.int32)
    selected_owner_device = jnp.sum(
        jnp.where(positions[None, :] == slot_index[:, None], owner[None, :], 0), 1
    )
    slot_energy = jnp.sum(
        jnp.where(positions[None, :] == selected_owner_device[:, None], energies[None, :], 0.0), 1
    )
    green, dos = sweep(slot_energy, places, hamil, hopping)
    return (green, dos)


def solution(mesh):
    in_specs = (
        P(("grp", "slab"), "orb", None),
        P(("grp", "slab"), None, "orb", None),
        P(("grp", "slab"), "orb", None),
        P(("grp", "slab"), None, "orb", None),
        P(("grp", "slab"), "orb", None),
        P(),
        P(),
    )
    out_specs = (P(("grp", "slab", "orb"), None, None, None), P(("grp", "slab", "orb"), None))
    return jax.shard_map(
        on_device, mesh=mesh, in_specs=in_specs, out_specs=out_specs, check_vma=False
    )
```

```python
import jax
import jax.numpy as jnp
from jax import lax
from jax.experimental import pallas as pl
from jax.experimental.pallas import tpu as pltpu
from jax.sharding import PartitionSpec as P

M = 256
BLK = 160
K = 8
NBLK = 32


broadening = 0.5
contact = 0.5


def shifted(array, axis, by):
    size = lax.axis_size(axis)
    return lax.ppermute(array, axis, [(i, (i + by) % size) for i in range(size)])


HALF = 128
TILES = HALF // 8


def spread(tile, index):
    return jnp.take_along_axis(tile, index, axis=1, mode="promise_in_bounds")


def invert_half(re, im):
    lane = lax.broadcasted_iota(jnp.int32, (8, HALF), 1)
    sub = lax.broadcasted_iota(jnp.int32, (8, HALF), 0)

    def eliminate(first, rows_re, rows_im):
        cols = []
        for j in range(8):
            index = jnp.full((8, HALF), first + j, jnp.int32)
            cols.append((spread(rows_re, index), spread(rows_im, index)))
        for j in range(8):
            at = lane == first + j
            here = sub == j
            col_re, col_im = cols[j]
            row_re = jnp.broadcast_to(rows_re[j : j + 1], (8, HALF))
            row_im = jnp.broadcast_to(rows_im[j : j + 1], (8, HALF))
            piv_re = jnp.broadcast_to(col_re[j : j + 1], (8, HALF))
            piv_im = jnp.broadcast_to(col_im[j : j + 1], (8, HALF))
            scale = 1.0 / (piv_re * piv_re + piv_im * piv_im)
            inv_re, inv_im = piv_re * scale, -piv_im * scale

            def reduced(old_re, old_im, row_re, row_im):
                new_re = row_re * inv_re - row_im * inv_im
                new_im = row_re * inv_im + row_im * inv_re
                rest_re = old_re - (col_re * new_re - col_im * new_im)
                rest_im = old_im - (col_re * new_im + col_im * new_re)
                return jnp.where(here, new_re, rest_re), jnp.where(here, new_im, rest_im)

            for m in range(j + 1, 8):
                old_re, old_im = cols[m]
                cols[m] = reduced(
                    old_re,
                    old_im,
                    jnp.broadcast_to(old_re[j : j + 1], (8, HALF)),
                    jnp.broadcast_to(old_im[j : j + 1], (8, HALF)),
                )
            rows_re, rows_im = reduced(
                jnp.where(at, 0.0, rows_re),
                jnp.where(at, 0.0, rows_im),
                jnp.where(at, 1.0, row_re),
                jnp.where(at, 0.0, row_im),
            )
        return rows_re, rows_im

    def update(first, old, panel):
        inside = (lane >= first) & (lane < first + 8)
        acc = [(jnp.where(inside, 0.0, a), jnp.where(inside, 0.0, b)) for a, b in old]
        for j in range(8):
            index = jnp.full((8, HALF), first + j, jnp.int32)
            row_re = jnp.broadcast_to(panel[0][j : j + 1], (8, HALF))
            row_im = jnp.broadcast_to(panel[1][j : j + 1], (8, HALF))
            for n in range(len(old)):
                col_re, col_im = spread(old[n][0], index), spread(old[n][1], index)
                acc[n] = (
                    acc[n][0] - col_re * row_re + col_im * row_im,
                    acc[n][1] - col_re * row_im - col_im * row_re,
                )
        return acc

    def block_step(block, panel):
        first = block * 8
        after = jnp.minimum(block + 1, TILES - 1)
        ahead = update(first, [(re[after], im[after])], panel)[0]
        following = eliminate(after * 8, *ahead)
        for part in range(0, TILES, 8):
            ids = range(part, part + 8)
            fresh = update(first, [(re[t], im[t]) for t in ids], panel)
            for n, t in enumerate(ids):
                re[t], im[t] = fresh[n]
        re[block], im[block] = panel
        return following

    lax.fori_loop(0, TILES, block_step, eliminate(0, re[0], im[0]))


def exact(left, right):
    return lax.dot_general(
        left,
        right,
        (((1,), (0,)), ((), ())),
        precision=lax.Precision.HIGHEST,
        preferred_element_type=jnp.float32,
    )


def times(left, right):
    width = right[0].shape[1]
    wide = jnp.concatenate([left[0], left[1]], 1)
    table = jnp.concatenate(
        [
            jnp.concatenate([right[0], right[1]], 1),
            jnp.concatenate([-right[1], right[0]], 1),
        ],
        0,
    )
    out = exact(wide, table)
    return out[:, :width], out[:, width:]


def adjoint(value):
    return value[0].T, -value[1].T


def sweep_kernel(energy_ref, places_ref, hamil_ref, hopping_ref, green_ref, dos_ref, work_re, work_im):
    eye = lax.broadcasted_iota(jnp.int32, (M, M), 0) == lax.broadcasted_iota(jnp.int32, (M, M), 1)
    energy = energy_ref[0]

    def inverse_of_half(re, im):
        work_re[...] = re.reshape(TILES, 8, HALF)
        work_im[...] = im.reshape(TILES, 8, HALF)
        invert_half(work_re, work_im)
        return work_re[...].reshape(HALF, HALF), work_im[...].reshape(HALF, HALF)

    def store(rows, columns, value):
        green_ref[0, rows, columns] = value[0]
        green_ref[1, rows, columns] = value[1]

    def load(rows, columns):
        return green_ref[0, rows, columns], green_ref[1, rows, columns]

    low, high = slice(0, HALF), slice(HALF, M)

    def step(s, _):
        lead = s == 0
        hop = places_ref[jnp.where(lead, hamil_ref.shape[0] - 1, s - 1)]
        here = places_ref[s]
        t = (hopping_ref[hop, 0], hopping_ref[hop, 1])
        t_adj = adjoint(t)

        @pl.when(lead)
        def _():
            wide = times(t_adj, t)
            green_ref[0] = contact * wide[1]
            green_ref[1] = -contact * wide[0]

        @pl.when(jnp.logical_not(lead))
        def _():
            self_energy = times(t_adj, times((green_ref[0], green_ref[1]), t))
            green_ref[0] = self_energy[0]
            green_ref[1] = self_energy[1]

        raw_re, raw_im = hamil_ref[here, 0], hamil_ref[here, 1]
        ham_re = (raw_re + raw_re.T) / 2.0
        ham_im = (raw_im - raw_im.T) / 2.0
        green_ref[0] = jnp.where(eye, energy, 0.0) - ham_re - green_ref[0]
        green_ref[1] = jnp.where(eye, broadening, 0.0) - ham_im - green_ref[1]

        corner = inverse_of_half(*load(low, low))
        store(low, low, corner)
        upper = times(corner, load(low, high))
        drop = times(load(high, low), upper)
        last = load(high, high)
        schur = inverse_of_half(last[0] - drop[0], last[1] - drop[1])
        corner = load(low, low)
        left = times(load(high, low), corner)
        bottom = times(schur, left)
        right = times(upper, schur)
        fill = times(upper, bottom)
        store(high, high, schur)
        store(high, low, (-bottom[0], -bottom[1]))
        store(low, high, (-right[0], -right[1]))
        store(low, low, (corner[0] + fill[0], corner[1] + fill[1]))
        dos_ref[s] = -jnp.sum(jnp.where(eye, green_ref[1], 0.0)) / M
        return 0

    lax.fori_loop(0, hamil_ref.shape[0], step, 0)


def sweep_one(energy, places, hamil, hopping):
    green, dos = pl.pallas_call(
        sweep_kernel,
        out_shape=(
            jax.ShapeDtypeStruct((2, M, M), jnp.float32),
            jax.ShapeDtypeStruct((hamil.shape[0],), jnp.float32),
        ),
        in_specs=[
            pl.BlockSpec(memory_space=pltpu.SMEM),
            pl.BlockSpec(memory_space=pltpu.SMEM),
            pl.BlockSpec(memory_space=pltpu.VMEM),
            pl.BlockSpec(memory_space=pltpu.VMEM),
        ],
        out_specs=(
            pl.BlockSpec(memory_space=pltpu.VMEM),
            pl.BlockSpec(memory_space=pltpu.SMEM),
        ),
        scratch_shapes=[pltpu.VMEM((TILES, 8, HALF), jnp.float32)] * 2,
        compiler_params=pltpu.CompilerParams(vmem_limit_bytes=40 * 1024 * 1024),
    )(energy.reshape(1), places, hamil, hopping)
    return green, dos


def sweep(energy, places, hamil, hopping):
    pairs = [sweep_one(energy[e], places, hamil, hopping) for e in range(energy.shape[0])]
    return jnp.stack([p[0] for p in pairs]), jnp.stack([p[1] for p in pairs])


def pick_blocks(table, index):
    return table[index]


def project(hamil, columns, mode_basis_row_block, basis_cols):
    slab_count = hamil.shape[0]
    row_count = hamil.shape[2]
    block_count = columns.shape[1]
    width = basis_cols.shape[2]
    table = basis_cols.reshape(slab_count, NBLK, BLK, width)
    chosen = jax.vmap(pick_blocks)(table, columns).reshape(slab_count, block_count, K * BLK, width)
    shaped = hamil.reshape(slab_count, 2, block_count, BLK, K * BLK)
    matrix_product_result = jnp.einsum(
        "scbrk,sbkm->scbrm", shaped, chosen, preferred_element_type=jnp.float32
    )
    matrix_product_result = matrix_product_result.astype(jnp.bfloat16).reshape(
        slab_count, 2, row_count, width
    )
    return jnp.einsum(
        "atw,abti->abwi",
        mode_basis_row_block,
        matrix_product_result,
        preferred_element_type=jnp.float32,
    )


def share(partial_value):
    slab_count = partial_value.shape[0]
    size = lax.axis_size("orb")
    if size <= 8:
        me = lax.axis_index("orb")
        pieces = partial_value.reshape(slab_count, size, 2 * M // size, M)

        def piece(which):
            return lax.dynamic_index_in_dim(pieces, lax.rem(which, size), 1, keepdims=True)

        own = piece(me)
        for by in [shifted(piece(me + k), "orb", k) for k in range(1, size)]:
            own = own + by
        moved = [own] + [shifted(own, "orb", k) for k in range(1, size)]
        summed = jnp.zeros_like(pieces)
        for k in range(size):
            place = lax.rem(me + size - k, size)
            summed = lax.dynamic_update_slice_in_dim(summed, moved[k], place, 1)
    else:
        summed = lax.psum(partial_value, "orb")
    blocks = summed.reshape(slab_count, 2, M, M)
    slabs = lax.axis_size("slab")
    if slabs & (slabs - 1):
        return lax.all_gather(blocks, "slab", axis=0, tiled=True)
    bit = slabs // 2
    while bit:
        other = lax.ppermute(blocks, "slab", [(i, i ^ bit) for i in range(slabs)])
        blocks = jnp.concatenate([blocks, other], 0)
        bit //= 2
    return blocks


def slab_places(slab_count):
    slabs = lax.axis_size("slab")
    device = jnp.arange(slabs, dtype=jnp.int32)
    if slabs & (slabs - 1) == 0:
        apart = device ^ lax.axis_index("slab")
        device = jnp.zeros_like(apart)
        bit, weight = slabs // 2, 1
        while bit:
            device = device + jnp.where((apart & bit) != 0, weight, 0)
            bit, weight = bit // 2, weight * 2
    inside = jnp.arange(slab_count, dtype=jnp.int32)
    return (device[:, None] * slab_count + inside[None, :]).reshape(-1)


def on_device(mode_basis, onsite, onsite_cols, coupling, coupling_cols, energies, owner):
    own_all = lax.all_gather(mode_basis, "orb", axis=1, tiled=True)
    following = []
    for first in (0, M // 2):
        half = own_all[:, :, first : first + M // 2]
        following.append(jnp.concatenate([half[1:], shifted(half[:1], "slab", -1)], 0))
    onsite_part = project(onsite, onsite_cols, mode_basis, own_all)
    hamil = share(onsite_part)
    coupling_part = jnp.concatenate(
        [project(coupling, coupling_cols, mode_basis, half) for half in following], -1
    )
    hopping = share(coupling_part)
    places = slab_places(mode_basis.shape[0])
    energy_count = energies.shape[0]
    per_device = energy_count // lax.axis_size(("slab", "orb"))
    slot_index = lax.axis_index(("slab", "orb")) * per_device + jnp.arange(
        per_device, dtype=jnp.int32
    )
    positions = jnp.arange(energy_count, dtype=jnp.int32)
    selected_owner_device = jnp.sum(
        jnp.where(positions[None, :] == slot_index[:, None], owner[None, :], 0), 1
    )
    slot_energy = jnp.sum(
        jnp.where(positions[None, :] == selected_owner_device[:, None], energies[None, :], 0.0), 1
    )
    green, dos = sweep(slot_energy, places, hamil, hopping)
    return (green, dos)


def solution(mesh):
    in_specs = (
        P(("grp", "slab"), "orb", None),
        P(("grp", "slab"), None, "orb", None),
        P(("grp", "slab"), "orb", None),
        P(("grp", "slab"), None, "orb", None),
        P(("grp", "slab"), "orb", None),
        P(),
        P(),
    )
    out_specs = (P(("grp", "slab", "orb"), None, None, None), P(("grp", "slab", "orb"), None))
    return jax.shard_map(
        on_device, mesh=mesh, in_specs=in_specs, out_specs=out_specs, check_vma=False
    )
```
